256 devices in a mesh: shard: 128 (over y, x, z_lo, core), rep: 2 (over z_hi).
Axes of the slice: x: 4, y: 4, z: 8 (z_hi: 2, z_lo: 4; z = z_hi * 4 + z_lo), core: 2. Of those that a mesh axis runs over, the one named last changes fastest.
Arguments:
- dense_feats: bfloat16 [32768, 13], P(('shard', 'rep')), may hold values from -6 to 6
- lookup_ids: int32 [32768, 13, 4], P(('shard', 'rep')), may hold values from 0 to 8191, as said below
- bag_lengths: int32 [32768, 13], P(('shard', 'rep')), may hold values from 1 to 4
- bottom_w1: bfloat16 [13, 512], replicated, may hold values from -1.75 to 1.75
- bottom_w2: bfloat16 [512, 256], replicated, may hold values from -0.25 to 0.25
- bottom_w3: bfloat16 [256, 128], replicated, may hold values from -0.375 to 0.375
- tables: bfloat16 [13, 8192, 128], P(None, 'shard'), may hold values from -3 to 3
- accum: float32 [13, 8192], P(None, 'shard'), may hold values from 0.05 to 1
- cross_down: bfloat16 [1792, 512], replicated, may hold values from -0.125 to 0.125
- cross_up: bfloat16 [512, 1792], replicated, may hold values from -0.25 to 0.25
- cross_bias: float32 [1792], replicated, may hold values from -3 to 3
- cotangent: bfloat16 [32768, 1792], P(('shard', 'rep')), may hold values from -0.3984375 to 0.3984375
Outputs:
- crossed: bfloat16 [32768, 1792], P(('shard', 'rep'))
- new_tables: float32 [13, 8192, 128], P(None, 'shard')
- new_accum: float32 [13, 8192], P(None, 'shard')
The draws below stay inside these ranges and needn't reach their ends.
Inputs may be any that keep to these rules, and one draw needn't show every extreme that they name: `lookup_ids`: row r of a table is held by index r // 64 of shard. Among the 6656 slots of one device (used or not), at most 78 name rows held by any one index of shard, and in every draw one index of shard gets exactly 78 from every device. Only the first bag_lengths[s, t] slots of bag (s, t) are used.
All inputs are finite; a program needn't handle non-finite values.
Results may differ from the reference program's by a relative error of at most 0.0065.
Values may be sent and summed in bfloat16 or wider, within the bound.
No kernel may reach another device: no remote copies, remote signals or barrier semaphores. Data moves between devices by JAX's collectives and lax.ppermute only.
A program may use at most 128 MiB of HBM per device.

```python
import math
import jax
import jax.numpy as jnp
from jax import lax

EMB = 128
NT = 13
DENSE = 13
H1 = 512
H2 = 256
RANK = 512
POOL = 4
B_DEV = 128
ROWS_DEV = 64
X = 1792
SAMPLES = 32768
ROWS = 8192
N_SHARD = 128
N_REP = 2


def draw_lookup_ids(key, part):
    block_count = N_SHARD * N_REP
    slot_count = B_DEV * NT * POOL
    mean_load = slot_count // N_SHARD
    half_load = mean_load // 2
    pair_count = N_SHARD // 2
    hot_key, rest_key = jax.random.split(jax.random.fold_in(key, 11))
    hottest = jax.random.randint(hot_key, (), 0, N_SHARD)

    def one_block(block_key):
        extra_key, label_key, shuffle_key, row_key = jax.random.split(block_key, 4)
        extra_load = jax.random.randint(extra_key, (pair_count,), 0, half_load + 1).at[0].set(half_load)
        counts = jnp.concatenate([mean_load + extra_load, mean_load - extra_load])
        labels = jax.random.permutation(label_key, N_SHARD)
        owner_of = (labels - labels[0] + hottest) % N_SHARD
        bounds = jnp.cumsum(counts)
        virtual = jnp.searchsorted(bounds, jnp.arange(slot_count), side='right')
        owners = jax.random.permutation(shuffle_key, owner_of[virtual])
        within_rows = jax.random.randint(row_key, (slot_count,), 0, ROWS_DEV)
        return (owners * ROWS_DEV + within_rows).reshape(B_DEV, NT, POOL)
    block_keys = jax.random.split(rest_key, block_count)
    return jax.vmap(one_block)(block_keys).reshape(B_DEV * block_count, NT, POOL).astype(jnp.int32)


def with_ends(drawn, rng, least, top_value):
    index_at = [jax.random.randint(jax.random.fold_in(rng, axis), (), 0, length) for axis, length in enumerate(drawn.shape)]
    longest = drawn.shape.index(max(drawn.shape))
    beside = index_at[:longest] + [(index_at[longest] + 1) % drawn.shape[longest]] + index_at[longest + 1:]
    return drawn.at[tuple(index_at)].set(least).at[tuple(beside)].set(top_value)


def levels(stream_key, shape, cuts, least, high):
    def one(position, parts):
        draws = jax.random.uniform(jax.random.fold_in(jax.random.fold_in(stream_key, 6), position), (parts,), jnp.float32, least / len(cuts), high / len(cuts))
        return jnp.repeat(jnp.exp(draws), shape[position] // parts).reshape((-1,) + (1,) * (len(shape) - position - 1))

    loudness = one(*cuts[0])
    for cut in cuts[1:]:
        loudness = loudness * one(*cut)
    return loudness


def noise(rng, extent, deviation, reach, cuts=(), kind=jnp.bfloat16):
    array = deviation * jax.random.normal(rng, extent, jnp.float32)
    if cuts:
        array = array * levels(rng, extent, cuts, -0.22, 0.18)
    return jnp.clip(array, -reach, reach).astype(kind)


def setup_inputs(seed: int = 0) -> dict:
    key_list = jax.random.split(jax.random.key(seed), 13)
    dense_feats = noise(key_list[0], (SAMPLES, DENSE), 1.0, 6.0, ((0, 256),))
    lookup_ids = draw_lookup_ids(jax.random.fold_in(key_list[12], 71), 0)
    bag_lengths = with_ends(jax.random.randint(key_list[2], (SAMPLES, NT), 1, POOL + 1), jax.random.fold_in(key_list[2], 1), 1, POOL).astype(jnp.int32)
    bottom_w1 = noise(key_list[3], (DENSE, H1), DENSE ** -0.5, 1.75)
    bottom_w2 = noise(key_list[4], (H1, H2), H1 ** -0.5, 0.25)
    bottom_w3 = noise(key_list[5], (H2, EMB), H2 ** -0.5, 0.375)
    tables = noise(key_list[6], (NT, ROWS, EMB), 0.5, 3.0, ((1, 128),))
    accum = jnp.clip(jnp.exp(math.log(1.0) - 2.9957323 * jax.random.uniform(key_list[7], (NT, ROWS), jnp.float32) ** levels(key_list[7], (NT, ROWS), ((1, 128),), -0.2, 0.2)), 0.05, 1.0)
    cross_down = noise(key_list[8], (X, RANK), X ** -0.5, 0.125)
    cross_up = noise(key_list[9], (RANK, X), RANK ** -0.5, 0.25)
    cross_bias = noise(key_list[10], (X,), 0.5, 3.0, (), jnp.float32)
    cotangent = noise(key_list[11], (SAMPLES, X), 0.05, 0.3984375, ((0, 256),))
    return dict(dense_feats=dense_feats, lookup_ids=lookup_ids, bag_lengths=bag_lengths, bottom_w1=bottom_w1, bottom_w2=bottom_w2, bottom_w3=bottom_w3, tables=tables, accum=accum, cross_down=cross_down, cross_up=cross_up, cross_bias=cross_bias, cotangent=cotangent)


step_size = 1.0
adagrad_eps = 1e-08

def cross_block(stacked, cross_down, cross_up, cross_bias, cotangent):
    low_rank = jnp.dot(stacked, cross_down, preferred_element_type=jnp.float32).astype(jnp.bfloat16)
    cross_hidden = jnp.dot(low_rank, cross_up, preferred_element_type=jnp.float32)
    widened = stacked.astype(jnp.float32)
    crossed = (widened * (cross_hidden + cross_bias) + widened).astype(jnp.bfloat16)
    cot_wide = cotangent.astype(jnp.float32)
    hidden_grad = (cot_wide * widened).astype(jnp.bfloat16)
    low_grad = jnp.dot(hidden_grad, cross_up.T, preferred_element_type=jnp.float32).astype(jnp.bfloat16)
    input_grad = cot_wide * (cross_hidden + cross_bias + 1.0) + jnp.dot(low_grad, cross_down.T, preferred_element_type=jnp.float32)
    return (crossed, input_grad)

def reference(dense_feats, lookup_ids, bag_lengths, bottom_w1, bottom_w2, bottom_w3, tables, accum, cross_down, cross_up, cross_bias, cotangent):
    blocks = N_SHARD * N_REP
    table_rows_flat = tables.reshape(NT * ROWS, EMB)
    offsets = (jnp.arange(NT, dtype=jnp.int32) * ROWS)[None, :, None]
    slot_index = jnp.arange(POOL, dtype=jnp.int32)[None, None, :]

    def one_block(running_total, piece_list):
        dense_slice, id_part, length_part, cot_part, block_index = piece_list
        live_mask = (slot_index < length_part[:, :, None]).astype(jnp.float32)
        flat_ids = (id_part + offsets).astype(jnp.int32)
        looked = table_rows_flat[flat_ids].astype(jnp.float32) * live_mask[..., None]
        pooled = lax.optimization_barrier(jnp.sum(looked, axis=2))
        first_layer = jax.nn.relu(jnp.dot(dense_slice, bottom_w1, preferred_element_type=jnp.float32)).astype(jnp.bfloat16)
        second_layer = jax.nn.relu(jnp.dot(first_layer, bottom_w2, preferred_element_type=jnp.float32)).astype(jnp.bfloat16)
        third_layer = jax.nn.relu(jnp.dot(second_layer, bottom_w3, preferred_element_type=jnp.float32)).astype(jnp.bfloat16)
        stacked = jnp.concatenate([third_layer, pooled.reshape(B_DEV, NT * EMB).astype(jnp.bfloat16)], axis=1)
        crossed, input_grad = cross_block(stacked, cross_down, cross_up, cross_bias, cot_part)
        pooled_grad = input_grad[:, EMB:].astype(jnp.bfloat16).reshape(B_DEV, NT, 1, EMB)
        entry_grad = pooled_grad.astype(jnp.float32) * live_mask[..., None]
        group_index = block_index % N_REP
        running_total = running_total.at[group_index, flat_ids.reshape(-1)].add(entry_grad.reshape(-1, EMB))
        return (running_total, crossed)
    piece_list = (dense_feats.reshape(blocks, B_DEV, DENSE), lookup_ids.reshape(blocks, B_DEV, NT, POOL), bag_lengths.reshape(blocks, B_DEV, NT), cotangent.reshape(blocks, B_DEV, X), jnp.arange(blocks, dtype=jnp.int32))
    initial = jnp.zeros((N_REP, NT * ROWS, EMB), jnp.float32)
    summed, crossed = lax.scan(one_block, initial, piece_list)
    rounded = lax.optimization_barrier(summed.astype(jnp.bfloat16)).astype(jnp.float32)
    row_grad = lax.optimization_barrier(jnp.sum(rounded, axis=0))
    new_accum = accum.reshape(-1) + lax.optimization_barrier(jnp.mean(row_grad * row_grad, axis=1))
    new_tables = table_rows_flat.astype(jnp.float32) - step_size * row_grad / (jnp.sqrt(new_accum)[:, None] + adagrad_eps)
    return (crossed.reshape(SAMPLES, X), new_tables.reshape(NT, ROWS, EMB), new_accum.reshape(NT, ROWS))
```

```python
import jax
import jax.numpy as jnp
from jax import lax
from jax.experimental import pallas as pl
from jax.experimental.pallas import tpu as pltpu
from jax.sharding import PartitionSpec as P

f32, bf16, i32 = jnp.float32, jnp.bfloat16, jnp.int32
step_size = 1.0
adagrad_eps = 1e-08

CORES = 2
Z_LO = 4
COLUMN = CORES * Z_LO
GROUPS = 16
SHARDS = COLUMN * GROUPS
REPS = 2
Z = Z_LO * REPS
EMB = 128
LANES = 128
POOL = 4
ROWS_DEV = 64
PIECE = GROUPS * ROWS_DEV
HALF = Z_LO * PIECE
ROWS = CORES * HALF

across = [[g * COLUMN + k for g in range(GROUPS)] for k in range(COLUMN)]
swap_cores = [(s, s ^ 1) for s in range(SHARDS)]


def along_z(step):
    pairs = []
    for s in range(SHARDS):
        place, z_lo, core = s // COLUMN, (s // CORES) % Z_LO, s % CORES
        for r in range(REPS):
            z = (r * Z_LO + z_lo + step) % Z
            target = place * COLUMN + (z % Z_LO) * CORES + core
            pairs.append((s * REPS + r, target * REPS + z // Z_LO))
    return pairs


def send_z(x, step):
    return lax.ppermute(x, ("shard", "rep"), along_z(step))


def exchange(x):
    return lax.all_to_all(
        x, "shard", split_axis=0, concat_axis=0, axis_index_groups=across, tiled=True
    )


vmem = pl.BlockSpec(memory_space=pltpu.VMEM)
smem = pl.BlockSpec(memory_space=pltpu.SMEM)


def lookup(ids, parts, unroll=32):
    count = len(parts)
    places, samples = GROUPS, ids.shape[1]

    def body(ids_ref, *refs):
        part_refs, (out_ref, tab, acc) = refs[:count], refs[count:]
        at = 0
        for ref in part_refs:
            tab[at : at + ref.shape[0], :] = ref[...].astype(f32)
            at += ref.shape[0]
        tab[at : at + 8, :] = jnp.zeros((8, EMB), f32)

        def place(g, _):
            def some(i, _):
                for u in range(unroll):
                    s = i * unroll + u
                    r = [tab[pl.ds(ids_ref[g * POOL + j, s], 1), :] for j in range(POOL)]
                    acc[pl.ds(g * samples + s, 1), :] = (r[0] + r[1]) + (r[2] + r[3])
                return 0

            return lax.fori_loop(0, samples // unroll, some, 0)

        lax.fori_loop(0, places, place, 0)
        out_ref[...] = acc[...].astype(bf16)

    return pl.pallas_call(
        body,
        out_shape=jax.ShapeDtypeStruct((places * samples, EMB), bf16),
        in_specs=[smem] + [vmem] * count,
        out_specs=vmem,
        scratch_shapes=[
            pltpu.VMEM((ROWS + 8, EMB), f32),
            pltpu.VMEM((places * samples, EMB), f32),
        ],
        compiler_params=pltpu.CompilerParams(vmem_limit_bytes=40 << 20),
        name="lookup",
    )(ids, *parts)


def scatter(ids, grads, unroll=16):
    places, samples = GROUPS, ids.shape[1]

    def body(ids_ref, grads_ref, keep_ref, send_ref, a0, a1, a2, a3, wide):
        accs = (a0, a1, a2, a3)
        for a in accs:
            a[...] = jnp.zeros((ROWS + 8, EMB), f32)
        wide[...] = grads_ref[...].astype(f32)

        def place(g, _):
            def some(i, _):
                for u in range(unroll):
                    s = i * unroll + u
                    row = wide[pl.ds(g * samples + s, 1), :]
                    at = [ids_ref[g * POOL + j, s] for j in range(POOL)]
                    v = [accs[j][pl.ds(at[j], 1), :] for j in range(POOL)]
                    v = [x + row for x in v]
                    for j in range(POOL):
                        accs[j][pl.ds(at[j], 1), :] = v[j]
                return 0

            return lax.fori_loop(0, samples // unroll, some, 0)

        lax.fori_loop(0, places, place, 0)
        block = 512

        def total(at):
            sl = pl.ds(pl.multiple_of(at, block), block)
            return (a0[sl, :] + a1[sl, :]) + (a2[sl, :] + a3[sl, :])

        def finish(i, _):
            sl = pl.ds(pl.multiple_of(i * block, block), block)
            send_ref[sl, :] = total(HALF + i * block).astype(bf16)
            keep_ref[sl, :] = total(i * block)
            return 0

        lax.fori_loop(0, HALF // block, finish, 0)

    return pl.pallas_call(
        body,
        out_shape=[
            jax.ShapeDtypeStruct((HALF, EMB), f32),
            jax.ShapeDtypeStruct((HALF, EMB), bf16),
        ],
        in_specs=[smem, vmem],
        out_specs=[vmem, vmem],
        scratch_shapes=[pltpu.VMEM((ROWS + 8, EMB), f32)] * POOL
        + [pltpu.VMEM((places * samples, EMB), f32)],
        compiler_params=pltpu.CompilerParams(vmem_limit_bytes=50 << 20),
        name="scatter",
    )(ids, grads)


contract_last = (((1,), (1,)), ((), ()))


def cross(dense, w1, w2, w3, pooled, down, up, bias, cot):
    rows, width = cot.shape
    tables = width // EMB - 1

    def body(
        dense_ref, w1_ref, w2_ref, w3_ref, pooled_ref, down_ref, up_ref, bias_ref, cot_ref,
        crossed_ref, grad_ref, stacked,
    ):
        def dot(a, b):
            return jnp.dot(a, b, preferred_element_type=f32)

        first = jax.nn.relu(dot(dense_ref[...], w1_ref[...])).astype(bf16)
        second = jax.nn.relu(dot(first, w2_ref[...])).astype(bf16)
        stacked[:, :EMB] = jax.nn.relu(dot(second, w3_ref[...])).astype(bf16)
        for t in range(tables):
            stacked[:, (t + 1) * EMB : (t + 2) * EMB] = pooled_ref[t]
        low_rank = dot(stacked[...], down_ref[...]).astype(bf16)
        hidden_grad = (cot_ref[...].astype(f32) * stacked[...].astype(f32)).astype(bf16)
        low_grad = lax.dot_general(
            hidden_grad, up_ref[...], contract_last, preferred_element_type=f32
        ).astype(bf16)
        for t in range(tables + 1):
            cols = slice(t * EMB, (t + 1) * EMB)
            hidden = dot(low_rank, up_ref[:, cols]) + bias_ref[:, cols]
            wide = stacked[:, cols].astype(f32)
            crossed_ref[:, cols] = (wide * hidden + wide).astype(bf16)
            if t > 0:
                back = lax.dot_general(
                    low_grad, down_ref[cols, :], contract_last, preferred_element_type=f32
                )
                grad_ref[t - 1] = (cot_ref[:, cols].astype(f32) * (hidden + 1.0) + back).astype(
                    bf16
                )
        for t in range(tables, GROUPS):
            grad_ref[t] = jnp.zeros((rows, EMB), bf16)

    return pl.pallas_call(
        body,
        out_shape=[
            jax.ShapeDtypeStruct((rows, width), bf16),
            jax.ShapeDtypeStruct((GROUPS, rows, EMB), bf16),
        ],
        in_specs=[vmem] * 9,
        out_specs=[vmem, vmem],
        scratch_shapes=[pltpu.VMEM((rows, width), bf16)],
        compiler_params=pltpu.CompilerParams(vmem_limit_bytes=40 << 20),
        name="cross",
    )(dense, w1, w2, w3, pooled, down, up, bias.reshape(1, width), cot)


def per_device(
    dense_feats,
    lookup_ids,
    bag_lengths,
    bottom_w1,
    bottom_w2,
    bottom_w3,
    tables,
    accum,
    cross_down,
    cross_up,
    cross_bias,
    cotangent,
):
    samples, table_count, pool = lookup_ids.shape
    me = lax.axis_index("shard")
    my_core, my_z = me % CORES, (me // CORES) % Z_LO

    ids = jnp.transpose(lookup_ids, (1, 2, 0))
    used = jnp.arange(pool, dtype=i32)[None, :, None] < bag_lengths.T[:, None, :]
    owner, row = ids >> 6, ids & 63
    place, owner_z, owner_core = owner >> 3, (owner >> 1) & 3, owner & 1
    address = (
        (owner_core ^ my_core) * HALF + ((owner_z - my_z) & 3) * PIECE + place * ROWS_DEV + row
    )
    address = jnp.where(used, address, ROWS)
    digits = jnp.concatenate([address >> 7, address & 127], axis=1).astype(f32).astype(bf16)
    payload = jnp.concatenate([tables, digits], axis=1)
    payload = jnp.pad(payload, ((0, GROUPS - table_count), (0, 0), (0, 0)))
    got = exchange(payload)
    own = got[:, :ROWS_DEV].reshape(PIECE, EMB)
    high, low = got[:, ROWS_DEV : ROWS_DEV + pool], got[:, ROWS_DEV + pool :]
    at = (high.astype(f32) * 128.0 + low.astype(f32)).astype(i32).reshape(GROUPS * pool, samples)

    mid = PIECE // 2
    pieces = [
        own,
        send_z(own, -1),
        send_z(own[:mid], -2),
        send_z(own[mid:], 2),
        send_z(own, 1),
    ]
    others = [lax.ppermute(x, "shard", swap_cores) for x in pieces]
    pooled = exchange(lookup(at, pieces + others).reshape(GROUPS, samples, EMB))

    crossed, pooled_grad = cross(
        dense_feats, bottom_w1, bottom_w2, bottom_w3, pooled, cross_down, cross_up, cross_bias,
        cotangent,
    )
    grads = exchange(pooled_grad).reshape(GROUPS * samples, EMB)
    keep, send = scatter(at, grads)
    both = keep + lax.ppermute(send, "shard", swap_cores).astype(f32)
    part = [both[d * PIECE : (d + 1) * PIECE] for d in range(Z_LO)]

    up, dn = part[0], part[1]
    for d in (3, 2, 1):
        up = send_z(up.astype(bf16), 1).astype(f32) + part[d]
    up = send_z(up.astype(bf16), 1).astype(f32)
    for d in (2, 3):
        dn = send_z(dn.astype(bf16), -1).astype(f32) + part[d]
    dn = send_z(dn.astype(bf16), -1).astype(f32)
    summed = (part[0] + up + dn).astype(bf16).reshape(GROUPS, ROWS_DEV, EMB)
    row_grad = exchange(summed)[:table_count].astype(f32)
    new_accum = accum + jnp.mean(row_grad * row_grad, axis=2)
    new_tables = tables.astype(f32) - step_size * row_grad / (
        jnp.sqrt(new_accum)[:, :, None] + adagrad_eps
    )
    return crossed, new_tables, new_accum


def solution(mesh):
    in_specs = (
        P(("shard", "rep"), None),
        P(("shard", "rep"), None, None),
        P(("shard", "rep"), None),
        P(),
        P(),
        P(),
        P(None, "shard", None),
        P(None, "shard"),
        P(),
        P(),
        P(),
        P(("shard", "rep"), None),
    )
    out_specs = (P(("shard", "rep"), None), P(None, "shard", None), P(None, "shard"))
    return jax.shard_map(
        per_device, mesh=mesh, in_specs=in_specs, out_specs=out_specs, check_vma=False
    )
```

```python
import jax
import jax.numpy as jnp
from jax import lax
from jax.experimental import pallas as pl
from jax.experimental.pallas import tpu as pltpu
from jax.sharding import PartitionSpec as P

f32, bf16, i32 = jnp.float32, jnp.bfloat16, jnp.int32
step_size = 1.0
adagrad_eps = 1e-08

CORES = 2
Z_LO = 4
COLUMN = CORES * Z_LO
GROUPS = 16
SHARDS = COLUMN * GROUPS
REPS = 2
Z = Z_LO * REPS
EMB = 128
LANES = 128
POOL = 4
ROWS_DEV = 64
PIECE = GROUPS * ROWS_DEV
HALF = Z_LO * PIECE
ROWS = CORES * HALF

across = [[g * COLUMN + k for g in range(GROUPS)] for k in range(COLUMN)]
across_reps = [[d * REPS + r for d in group for r in range(REPS)] for group in across]
swap_cores = [(s, s ^ 1) for s in range(SHARDS)]


def along_z(step):
    pairs = []
    for s in range(SHARDS):
        place, z_lo, core = s // COLUMN, (s // CORES) % Z_LO, s % CORES
        for r in range(REPS):
            z = (r * Z_LO + z_lo + (step if core == 0 else -step)) % Z
            target = place * COLUMN + (z % Z_LO) * CORES + core
            pairs.append((s * REPS + r, target * REPS + z // Z_LO))
    return pairs


def send_z(x, step):
    return lax.ppermute(x, ("shard", "rep"), along_z(step))


def swap(x):
    return lax.ppermute(x, "shard", swap_cores)


def exchange(x):
    return lax.all_to_all(
        x, "shard", split_axis=0, concat_axis=0, axis_index_groups=across, tiled=True
    )


def exchange_reps(x):
    return lax.all_to_all(
        x,
        ("shard", "rep"),
        split_axis=0,
        concat_axis=0,
        axis_index_groups=across_reps,
        tiled=True,
    )


vmem = pl.BlockSpec(memory_space=pltpu.VMEM)
smem = pl.BlockSpec(memory_space=pltpu.SMEM)


def lookup(ids, parts, samples, unroll=32):
    count = len(parts)
    places = GROUPS

    def body(ids_ref, *refs):
        part_refs, (out_ref, tab, acc) = refs[:count], refs[count:]
        at = 0
        for ref in part_refs:
            tab[at : at + ref.shape[0], :] = ref[...].astype(f32)
            at += ref.shape[0]
        tab[at : at + 8, :] = jnp.zeros((8, EMB), f32)

        def place(g, _):
            def some(i, _):
                base = g * (POOL * samples) + i * unroll
                bag = g * samples + i * unroll
                for u in range(unroll):
                    r = [
                        tab[pl.ds(ids_ref[base + (j * samples + u)], 1), :] for j in range(POOL)
                    ]
                    acc[pl.ds(bag + u, 1), :] = (r[0] + r[1]) + (r[2] + r[3])
                return 0

            return lax.fori_loop(0, samples // unroll, some, 0)

        lax.fori_loop(0, places, place, 0)
        out_ref[...] = acc[...].astype(bf16)

    return pl.pallas_call(
        body,
        out_shape=jax.ShapeDtypeStruct((places * samples, EMB), bf16),
        in_specs=[smem] + [vmem] * count,
        out_specs=vmem,
        scratch_shapes=[
            pltpu.VMEM((ROWS + 8, EMB), f32),
            pltpu.VMEM((places * samples, EMB), f32),
        ],
        compiler_params=pltpu.CompilerParams(vmem_limit_bytes=24 << 20),
        name="lookup",
    )(ids, *parts)


def scatter(ids, grads, samples, unroll=16):
    places, pair = GROUPS, 2
    totals = pair * POOL

    def body(ids_ref, grads_ref, keep_ref, send_ref, *scratch):
        accs, wide = scratch[:totals], scratch[totals]
        for a in accs:
            a[...] = jnp.zeros((ROWS + 8, EMB), f32)
        wide[...] = grads_ref[...].astype(f32)

        def place(g, _):
            def some(i, _):
                base = g * (POOL * samples) + i * unroll
                bag = g * samples + i * unroll
                for u in range(0, unroll, pair):
                    row = [wide[pl.ds(bag + (u + k), 1), :] for k in range(pair)]
                    at = [
                        ids_ref[base + (j * samples + u + k)]
                        for k in range(pair)
                        for j in range(POOL)
                    ]
                    new = [
                        accs[n][pl.ds(at[n], 1), :] + row[n // POOL] for n in range(totals)
                    ]
                    for n in range(totals):
                        accs[n][pl.ds(at[n], 1), :] = new[n]
                return 0

            return lax.fori_loop(0, samples // unroll, some, 0)

        lax.fori_loop(0, places, place, 0)
        block = 256

        def total(at):
            sl = pl.ds(pl.multiple_of(at, block), block)
            t = [a[sl, :] for a in accs]
            while len(t) > 1:
                t = [t[2 * k] + t[2 * k + 1] for k in range(len(t) // 2)]
            return t[0]

        def finish(i, _):
            sl = pl.ds(pl.multiple_of(i * block, block), block)
            send_ref[sl, :] = total(HALF + i * block).astype(bf16)
            keep_ref[sl, :] = total(i * block)
            return 0

        lax.fori_loop(0, HALF // block, finish, 0)

    return pl.pallas_call(
        body,
        out_shape=[
            jax.ShapeDtypeStruct((HALF, EMB), f32),
            jax.ShapeDtypeStruct((HALF, EMB), bf16),
        ],
        in_specs=[smem, vmem],
        out_specs=[vmem, vmem],
        scratch_shapes=[pltpu.VMEM((ROWS + 8, EMB), f32)] * totals
        + [pltpu.VMEM((places * samples, EMB), f32)],
        compiler_params=pltpu.CompilerParams(vmem_limit_bytes=44 << 20),
        name="scatter",
    )(ids, grads)


contract_last = (((1,), (1,)), ((), ()))


def cross(dense, w1, w2, w3, pooled, down, up, bias, cot):
    rows, width = cot.shape
    tables = width // EMB - 1

    def body(
        dense_ref, w1_ref, w2_ref, w3_ref, pooled_ref, down_ref, up_ref, bias_ref, cot_ref,
        crossed_ref, grad_ref, stacked,
    ):
        def dot(a, b):
            return jnp.dot(a, b, preferred_element_type=f32)

        first = jax.nn.relu(dot(dense_ref[...], w1_ref[...])).astype(bf16)
        second = jax.nn.relu(dot(first, w2_ref[...])).astype(bf16)
        stacked[:, :EMB] = jax.nn.relu(dot(second, w3_ref[...])).astype(bf16)
        for t in range(tables):
            stacked[:, (t + 1) * EMB : (t + 2) * EMB] = pooled_ref[t]
        low_rank = dot(stacked[...], down_ref[...]).astype(bf16)
        hidden_grad = (cot_ref[...].astype(f32) * stacked[...].astype(f32)).astype(bf16)
        low_grad = lax.dot_general(
            hidden_grad, up_ref[...], contract_last, preferred_element_type=f32
        ).astype(bf16)
        for t in range(tables + 1):
            cols = slice(t * EMB, (t + 1) * EMB)
            hidden = dot(low_rank, up_ref[:, cols]) + bias_ref[:, cols]
            wide = stacked[:, cols].astype(f32)
            crossed_ref[:, cols] = (wide * hidden + wide).astype(bf16)
            if t > 0:
                back = lax.dot_general(
                    low_grad, down_ref[cols, :], contract_last, preferred_element_type=f32
                )
                grad_ref[t - 1] = (cot_ref[:, cols].astype(f32) * (hidden + 1.0) + back).astype(
                    bf16
                )
        for t in range(tables, GROUPS):
            grad_ref[t] = jnp.zeros((rows, EMB), bf16)

    return pl.pallas_call(
        body,
        out_shape=[
            jax.ShapeDtypeStruct((rows, width), bf16),
            jax.ShapeDtypeStruct((GROUPS, rows, EMB), bf16),
        ],
        in_specs=[vmem] * 9,
        out_specs=[vmem, vmem],
        scratch_shapes=[pltpu.VMEM((rows, width), bf16)],
        compiler_params=pltpu.CompilerParams(vmem_limit_bytes=20 << 20),
        name="cross",
    )(dense, w1, w2, w3, pooled, down, up, bias.reshape(1, width), cot)


def per_device(
    dense_feats,
    lookup_ids,
    bag_lengths,
    bottom_w1,
    bottom_w2,
    bottom_w3,
    tables,
    accum,
    cross_down,
    cross_up,
    cross_bias,
    cotangent,
):
    samples, table_count, pool = lookup_ids.shape
    me = lax.axis_index("shard")
    my_core, my_z = me % CORES, (me // CORES) % Z_LO

    ids = jnp.transpose(lookup_ids, (1, 2, 0))
    used = jnp.arange(pool, dtype=i32)[None, :, None] < bag_lengths.T[:, None, :]
    owner, row = ids >> 6, ids & 63
    place, owner_z, owner_core = owner >> 3, (owner >> 1) & 3, owner & 1
    steps = ((owner_z - my_z) * (1 - 2 * my_core)) & 3
    address = (owner_core ^ my_core) * HALF + steps * PIECE + place * ROWS_DEV + row
    address = jnp.where(used, address, ROWS)
    digits = jnp.concatenate([address >> 7, address & 127], axis=1).astype(f32).astype(bf16)
    payload = jnp.concatenate([tables, digits], axis=1)
    payload = jnp.pad(payload, ((0, GROUPS - table_count), (0, 0), (0, 0)))
    got = exchange(payload)
    own = got[:, :ROWS_DEV].reshape(PIECE, EMB)
    high, low = got[:, ROWS_DEV : ROWS_DEV + pool], got[:, ROWS_DEV + pool :]
    at = (high.astype(f32) * 128.0 + low.astype(f32)).astype(i32).reshape(-1)

    two = send_z(own, -2)
    one, three = send_z(own, -1), send_z(own, 1)
    pieces = [own, one, two, three] + [swap(x) for x in (own, three, two, one)]
    pooled = exchange(lookup(at, pieces, samples).reshape(GROUPS, samples, EMB))

    crossed, pooled_grad = cross(
        dense_feats, bottom_w1, bottom_w2, bottom_w3, pooled, cross_down, cross_up, cross_bias,
        cotangent,
    )
    grads = exchange(pooled_grad).reshape(GROUPS * samples, EMB)
    keep, send = scatter(at, grads, samples)
    theirs = swap(send).reshape(Z_LO, PIECE, EMB)
    keep = keep.reshape(Z_LO, PIECE, EMB)

    def chip(d):
        return keep[d] + theirs[-d % Z_LO].astype(f32)

    far = send_z(chip(2).astype(bf16), -1)
    below = send_z(chip(1).astype(bf16), 1)
    above = send_z((chip(3) + far.astype(f32)).astype(bf16), -1)
    summed = (chip(0) + below.astype(f32) + above.astype(f32)).astype(bf16)
    summed = summed.reshape(GROUPS, 1, ROWS_DEV, EMB)
    halves = exchange_reps(
        jnp.broadcast_to(summed, (GROUPS, REPS, ROWS_DEV, EMB)).reshape(-1, ROWS_DEV, EMB)
    ).reshape(GROUPS, REPS, ROWS_DEV, EMB)[:table_count]
    row_grad = halves.astype(f32).sum(axis=1)
    new_accum = accum + jnp.mean(row_grad * row_grad, axis=2)
    new_tables = tables.astype(f32) - step_size * row_grad / (
        jnp.sqrt(new_accum)[:, :, None] + adagrad_eps
    )
    return crossed, new_tables, new_accum


def solution(mesh):
    in_specs = (
        P(("shard", "rep"), None),
        P(("shard", "rep"), None, None),
        P(("shard", "rep"), None),
        P(),
        P(),
        P(),
        P(None, "shard", None),
        P(None, "shard"),
        P(),
        P(),
        P(),
        P(("shard", "rep"), None),
    )
    out_specs = (P(("shard", "rep"), None), P(None, "shard", None), P(None, "shard"))
    return jax.shard_map(
        per_device, mesh=mesh, in_specs=in_specs, out_specs=out_specs, check_vma=False
    )
```

```python
import jax
import jax.numpy as jnp
from jax import lax
from jax.experimental import pallas as pl
from jax.experimental.pallas import tpu as pltpu
from jax.sharding import PartitionSpec as P

f32, bf16, i32 = jnp.float32, jnp.bfloat16, jnp.int32
step_size = 1.0
adagrad_eps = 1e-08

CORES = 2
Z_LO = 4
COLUMN = CORES * Z_LO
GROUPS = 16
SHARDS = COLUMN * GROUPS
REPS = 2
Z = Z_LO * REPS
EMB = 128
LANES = 128
POOL = 4
ROWS_DEV = 64
PIECE = GROUPS * ROWS_DEV
HALF = Z_LO * PIECE
ROWS = CORES * HALF

across = [[g * COLUMN + k for g in range(GROUPS)] for k in range(COLUMN)]
across_reps = [[d * REPS + r for d in group for r in range(REPS)] for group in across]
swap_cores = [(s, s ^ 1) for s in range(SHARDS)]


def along_z(step):
    pairs = []
    for s in range(SHARDS):
        place, z_lo, core = s // COLUMN, (s // CORES) % Z_LO, s % CORES
        for r in range(REPS):
            z = (r * Z_LO + z_lo + (step if core == 0 else -step)) % Z
            target = place * COLUMN + (z % Z_LO) * CORES + core
            pairs.append((s * REPS + r, target * REPS + z // Z_LO))
    return pairs


def send_z(x, step):
    return lax.ppermute(x, ("shard", "rep"), along_z(step))


def swap(x):
    return lax.ppermute(x, "shard", swap_cores)


def exchange(x):
    return lax.all_to_all(
        x, "shard", split_axis=0, concat_axis=0, axis_index_groups=across, tiled=True
    )


def exchange_reps(x):
    return lax.all_to_all(
        x,
        ("shard", "rep"),
        split_axis=0,
        concat_axis=0,
        axis_index_groups=across_reps,
        tiled=True,
    )


vmem = pl.BlockSpec(memory_space=pltpu.VMEM)
anywhere = pl.BlockSpec(memory_space=pl.ANY)


def lookup(ids, parts, samples, unroll=32):
    count = len(parts)
    places = GROUPS

    def body(ids_any, *refs):
        part_refs, (out_ref, tab, acc, ids_ref, sem) = refs[:count], refs[count:]
        copy = pltpu.make_async_copy(ids_any, ids_ref, sem)
        copy.start()
        at = 0
        for ref in part_refs:
            tab[at : at + ref.shape[0], :] = ref[...].astype(f32)
            at += ref.shape[0]
        tab[at : at + 8, :] = jnp.zeros((8, EMB), f32)
        copy.wait()

        def place(g, _):
            def some(i, _):
                base = g * (POOL * samples) + i * unroll
                bag = g * samples + i * unroll
                for u in range(unroll):
                    r = [
                        tab[pl.ds(ids_ref[base + (j * samples + u)], 1), :] for j in range(POOL)
                    ]
                    acc[pl.ds(bag + u, 1), :] = (r[0] + r[1]) + (r[2] + r[3])
                return 0

            return lax.fori_loop(0, samples // unroll, some, 0)

        lax.fori_loop(0, places, place, 0)
        out_ref[...] = acc[...].astype(bf16)

    return pl.pallas_call(
        body,
        out_shape=jax.ShapeDtypeStruct((places * samples, EMB), bf16),
        in_specs=[anywhere] + [vmem] * count,
        out_specs=vmem,
        scratch_shapes=[
            pltpu.VMEM((ROWS + 8, EMB), f32),
            pltpu.VMEM((places * samples, EMB), f32),
            pltpu.SMEM((places * POOL * samples,), i32),
            pltpu.SemaphoreType.DMA,
        ],
        compiler_params=pltpu.CompilerParams(vmem_limit_bytes=10 << 20),
        name="lookup",
    )(ids, *parts)


def scatter(ids, grads, samples, unroll=16):
    places, pair = GROUPS, 2
    totals = pair * POOL

    def body(ids_any, grads_ref, keep_ref, send_ref, *scratch):
        accs, (wide, ids_ref, sem) = scratch[:totals], scratch[totals:]
        copy = pltpu.make_async_copy(ids_any, ids_ref, sem)
        copy.start()
        for a in accs:
            a[...] = jnp.zeros((ROWS + 8, EMB), f32)
        wide[...] = grads_ref[...].astype(f32)
        copy.wait()

        def place(g, _):
            def some(i, _):
                base = g * (POOL * samples) + i * unroll
                bag = g * samples + i * unroll
                for u in range(0, unroll, pair):
                    row = [wide[pl.ds(bag + (u + k), 1), :] for k in range(pair)]
                    at = [
                        ids_ref[base + (j * samples + u + k)]
                        for k in range(pair)
                        for j in range(POOL)
                    ]
                    new = [
                        accs[n][pl.ds(at[n], 1), :] + row[n // POOL] for n in range(totals)
                    ]
                    for n in range(totals):
                        accs[n][pl.ds(at[n], 1), :] = new[n]
                return 0

            return lax.fori_loop(0, samples // unroll, some, 0)

        lax.fori_loop(0, places, place, 0)
        block = 256

        def total(at):
            sl = pl.ds(pl.multiple_of(at, block), block)
            t = [a[sl, :] for a in accs]
            while len(t) > 1:
                t = [t[2 * k] + t[2 * k + 1] for k in range(len(t) // 2)]
            return t[0]

        def finish(i, _):
            sl = pl.ds(pl.multiple_of(i * block, block), block)
            send_ref[sl, :] = total(HALF + i * block).astype(bf16)
            keep_ref[sl, :] = total(i * block)
            return 0

        lax.fori_loop(0, HALF // block, finish, 0)

    return pl.pallas_call(
        body,
        out_shape=[
            jax.ShapeDtypeStruct((HALF, EMB), f32),
            jax.ShapeDtypeStruct((HALF, EMB), bf16),
        ],
        in_specs=[anywhere, vmem],
        out_specs=[vmem, vmem],
        scratch_shapes=[pltpu.VMEM((ROWS + 8, EMB), f32)] * totals
        + [
            pltpu.VMEM((places * samples, EMB), f32),
            pltpu.SMEM((places * POOL * samples,), i32),
            pltpu.SemaphoreType.DMA,
        ],
        compiler_params=pltpu.CompilerParams(vmem_limit_bytes=38 << 20),
        name="scatter",
    )(ids, grads)


contract_last = (((1,), (1,)), ((), ()))


def dot(a, b):
    return jnp.dot(a, b, preferred_element_type=f32)


def bottom(dense, w1, w2, w3):
    def body(dense_ref, w1_ref, w2_ref, w3_ref, out_ref):
        first = jax.nn.relu(dot(dense_ref[...], w1_ref[...])).astype(bf16)
        second = jax.nn.relu(dot(first, w2_ref[...])).astype(bf16)
        out_ref[...] = jax.nn.relu(dot(second, w3_ref[...])).astype(bf16)

    return pl.pallas_call(
        body,
        out_shape=jax.ShapeDtypeStruct((dense.shape[0], EMB), bf16),
        in_specs=[vmem] * 4,
        out_specs=vmem,
        compiler_params=pltpu.CompilerParams(vmem_limit_bytes=4 << 20),
        name="bottom",
    )(dense, w1, w2, w3)


def cross(third, pooled, down, up, bias, cot):
    rows, width = cot.shape
    tables = width // EMB - 1

    def body(
        third_ref, pooled_ref, down_ref, up_ref, bias_ref, cot_ref, crossed_ref, grad_ref, stacked
    ):
        stacked[:, :EMB] = third_ref[...]
        for t in range(tables):
            stacked[:, (t + 1) * EMB : (t + 2) * EMB] = pooled_ref[t]
        low_rank = dot(stacked[...], down_ref[...]).astype(bf16)
        hidden_grad = (cot_ref[...].astype(f32) * stacked[...].astype(f32)).astype(bf16)
        low_grad = lax.dot_general(
            hidden_grad, up_ref[...], contract_last, preferred_element_type=f32
        ).astype(bf16)
        for t in range(tables + 1):
            cols = slice(t * EMB, (t + 1) * EMB)
            hidden = dot(low_rank, up_ref[:, cols]) + bias_ref[:, cols]
            wide = stacked[:, cols].astype(f32)
            crossed_ref[:, cols] = (wide * hidden + wide).astype(bf16)
            if t > 0:
                back = lax.dot_general(
                    low_grad, down_ref[cols, :], contract_last, preferred_element_type=f32
                )
                grad_ref[t - 1] = (cot_ref[:, cols].astype(f32) * (hidden + 1.0) + back).astype(
                    bf16
                )
        for t in range(tables, GROUPS):
            grad_ref[t] = jnp.zeros((rows, EMB), bf16)

    return pl.pallas_call(
        body,
        out_shape=[
            jax.ShapeDtypeStruct((rows, width), bf16),
            jax.ShapeDtypeStruct((GROUPS, rows, EMB), bf16),
        ],
        in_specs=[vmem] * 6,
        out_specs=[vmem, vmem],
        scratch_shapes=[pltpu.VMEM((rows, width), bf16)],
        compiler_params=pltpu.CompilerParams(vmem_limit_bytes=6 << 20),
        name="cross",
    )(third, pooled, down, up, bias.reshape(1, width), cot)


def per_device(
    dense_feats,
    lookup_ids,
    bag_lengths,
    bottom_w1,
    bottom_w2,
    bottom_w3,
    tables,
    accum,
    cross_down,
    cross_up,
    cross_bias,
    cotangent,
):
    samples, table_count, pool = lookup_ids.shape
    me = lax.axis_index("shard")
    my_core, my_z = me % CORES, (me // CORES) % Z_LO

    ids = jnp.transpose(lookup_ids, (1, 2, 0))
    used = jnp.arange(pool, dtype=i32)[None, :, None] < bag_lengths.T[:, None, :]
    owner, row = ids >> 6, ids & 63
    place, owner_z, owner_core = owner >> 3, (owner >> 1) & 3, owner & 1
    steps = ((owner_z - my_z) * (1 - 2 * my_core)) & 3
    address = (owner_core ^ my_core) * HALF + steps * PIECE + place * ROWS_DEV + row
    address = jnp.where(used, address, ROWS)
    digits = jnp.concatenate([address >> 7, address & 127], axis=1).astype(f32).astype(bf16)
    payload = jnp.concatenate([tables, digits], axis=1)
    payload = jnp.pad(payload, ((0, GROUPS - table_count), (0, 0), (0, 0)))
    got = exchange(payload)
    own = got[:, :ROWS_DEV].reshape(PIECE, EMB)
    high, low = got[:, ROWS_DEV : ROWS_DEV + pool], got[:, ROWS_DEV + pool :]
    at = (high.astype(f32) * 128.0 + low.astype(f32)).astype(i32).reshape(-1)

    one, three = send_z(own, -1), send_z(own, 1)
    two = send_z(one, -1)
    pieces = [own, one, two, three] + [swap(x) for x in (own, three, two, one)]
    pooled = exchange(lookup(at, pieces, samples).reshape(GROUPS, samples, EMB))

    crossed, pooled_grad = cross(
        bottom(dense_feats, bottom_w1, bottom_w2, bottom_w3),
        pooled,
        cross_down,
        cross_up,
        cross_bias,
        cotangent,
    )
    grads = exchange(pooled_grad).reshape(GROUPS * samples, EMB)
    keep, send = scatter(at, grads, samples)
    theirs = swap(send).reshape(Z_LO, PIECE, EMB)
    keep = keep.reshape(Z_LO, PIECE, EMB)

    def chip(d):
        return keep[d] + theirs[-d % Z_LO].astype(f32)

    far = send_z(chip(2).astype(bf16), -1)
    below = send_z(chip(1).astype(bf16), 1)
    above = send_z((chip(3) + far.astype(f32)).astype(bf16), -1)
    summed = (chip(0) + below.astype(f32) + above.astype(f32)).astype(bf16)
    summed = summed.reshape(GROUPS, 1, ROWS_DEV, EMB)
    halves = exchange_reps(
        jnp.broadcast_to(summed, (GROUPS, REPS, ROWS_DEV, EMB)).reshape(-1, ROWS_DEV, EMB)
    ).reshape(GROUPS, REPS, ROWS_DEV, EMB)[:table_count]
    row_grad = halves.astype(f32).sum(axis=1)
    new_accum = accum + jnp.mean(row_grad * row_grad, axis=2)
    new_tables = tables.astype(f32) - step_size * row_grad / (
        jnp.sqrt(new_accum)[:, :, None] + adagrad_eps
    )
    return crossed, new_tables, new_accum


def solution(mesh):
    in_specs = (
        P(("shard", "rep"), None),
        P(("shard", "rep"), None, None),
        P(("shard", "rep"), None),
        P(),
        P(),
        P(),
        P(None, "shard", None),
        P(None, "shard"),
        P(),
        P(),
        P(),
        P(("shard", "rep"), None),
    )
    out_specs = (P(("shard", "rep"), None), P(None, "shard", None), P(None, "shard"))
    return jax.shard_map(
        per_device, mesh=mesh, in_specs=in_specs, out_specs=out_specs, check_vma=False
    )
```

```python
import jax
import jax.numpy as jnp
from jax import lax
from jax.experimental import pallas as pl
from jax.experimental.pallas import tpu as pltpu
from jax.sharding import PartitionSpec as P

f32, bf16, i32 = jnp.float32, jnp.bfloat16, jnp.int32
step_size = 1.0
adagrad_eps = 1e-08

CORES = 2
Z_LO = 4
COLUMN = CORES * Z_LO
GROUPS = 16
SHARDS = COLUMN * GROUPS
REPS = 2
Z = Z_LO * REPS
EMB = 128
LANES = 128
POOL = 4
ROWS_DEV = 64
PIECE = GROUPS * ROWS_DEV
HALF = Z_LO * PIECE
ROWS = CORES * HALF

across = [[g * COLUMN + k for g in range(GROUPS)] for k in range(COLUMN)]
across_reps = [[d * REPS + r for d in group for r in range(REPS)] for group in across]
swap_cores = [(s, s ^ 1) for s in range(SHARDS)]


def along_z(step):
    pairs = []
    for s in range(SHARDS):
        place, z_lo, core = s // COLUMN, (s // CORES) % Z_LO, s % CORES
        for r in range(REPS):
            z = (r * Z_LO + z_lo + (step if core == 0 else -step)) % Z
            target = place * COLUMN + (z % Z_LO) * CORES + core
            pairs.append((s * REPS + r, target * REPS + z // Z_LO))
    return pairs


def send_z(x, step):
    return lax.ppermute(x, ("shard", "rep"), along_z(step))


def swap(x):
    return lax.ppermute(x, "shard", swap_cores)


def exchange(x):
    return lax.all_to_all(
        x, "shard", split_axis=0, concat_axis=0, axis_index_groups=across, tiled=True
    )


def exchange_reps(x):
    return lax.all_to_all(
        x,
        ("shard", "rep"),
        split_axis=0,
        concat_axis=0,
        axis_index_groups=across_reps,
        tiled=True,
    )


vmem = pl.BlockSpec(memory_space=pltpu.VMEM)
anywhere = pl.BlockSpec(memory_space=pl.ANY)


def lookup(ids, parts, samples, unroll=128):
    count = len(parts)
    places = GROUPS

    def body(ids_any, *refs):
        part_refs, (out_ref, tab, acc, ids_ref, sem) = refs[:count], refs[count:]
        copy = pltpu.make_async_copy(ids_any, ids_ref, sem)
        copy.start()
        at = 0
        for ref in part_refs:
            tab[at : at + ref.shape[0], :] = ref[...].astype(f32)
            at += ref.shape[0]
        tab[at : at + 8, :] = jnp.zeros((8, EMB), f32)
        copy.wait()

        def place(g, _):
            def some(i, _):
                base = g * (POOL * samples) + i * unroll
                bag = g * samples + i * unroll
                for u in range(unroll):
                    r = [
                        tab[pl.ds(ids_ref[base + (j * samples + u)], 1), :] for j in range(POOL)
                    ]
                    acc[pl.ds(bag + u, 1), :] = (r[0] + r[1]) + (r[2] + r[3])
                return 0

            return lax.fori_loop(0, samples // unroll, some, 0)

        lax.fori_loop(0, places, place, 0)
        out_ref[...] = acc[...].astype(bf16)

    return pl.pallas_call(
        body,
        out_shape=jax.ShapeDtypeStruct((places * samples, EMB), bf16),
        in_specs=[anywhere] + [vmem] * count,
        out_specs=vmem,
        scratch_shapes=[
            pltpu.VMEM((ROWS + 8, EMB), f32),
            pltpu.VMEM((places * samples, EMB), f32),
            pltpu.SMEM((places * POOL * samples,), i32),
            pltpu.SemaphoreType.DMA,
        ],
        compiler_params=pltpu.CompilerParams(vmem_limit_bytes=10 << 20),
        name="lookup",
    )(ids, *parts)


def scatter(ids, grads, samples, unroll=64):
    places, pair = GROUPS, 2
    totals = pair * POOL

    def body(ids_any, grads_ref, keep_ref, send_ref, *scratch):
        accs, (wide, ids_ref, sem) = scratch[:totals], scratch[totals:]
        copy = pltpu.make_async_copy(ids_any, ids_ref, sem)
        copy.start()
        for a in accs:
            a[...] = jnp.zeros((ROWS + 8, EMB), f32)
        wide[...] = grads_ref[...].astype(f32)
        copy.wait()

        def place(g, _):
            def some(i, _):
                base = g * (POOL * samples) + i * unroll
                bag = g * samples + i * unroll
                for u in range(0, unroll, pair):
                    row = [wide[pl.ds(bag + (u + k), 1), :] for k in range(pair)]
                    at = [
                        ids_ref[base + (j * samples + u + k)]
                        for k in range(pair)
                        for j in range(POOL)
                    ]
                    new = [
                        accs[n][pl.ds(at[n], 1), :] + row[n // POOL] for n in range(totals)
                    ]
                    for n in range(totals):
                        accs[n][pl.ds(at[n], 1), :] = new[n]
                return 0

            return lax.fori_loop(0, samples // unroll, some, 0)

        lax.fori_loop(0, places, place, 0)
        block = 256

        def total(at):
            sl = pl.ds(pl.multiple_of(at, block), block)
            t = [a[sl, :] for a in accs]
            while len(t) > 1:
                t = [t[2 * k] + t[2 * k + 1] for k in range(len(t) // 2)]
            return t[0]

        def finish(i, _):
            sl = pl.ds(pl.multiple_of(i * block, block), block)
            send_ref[sl, :] = total(HALF + i * block).astype(bf16)
            keep_ref[sl, :] = total(i * block)
            return 0

        lax.fori_loop(0, HALF // block, finish, 0)

    return pl.pallas_call(
        body,
        out_shape=[
            jax.ShapeDtypeStruct((HALF, EMB), f32),
            jax.ShapeDtypeStruct((HALF, EMB), bf16),
        ],
        in_specs=[anywhere, vmem],
        out_specs=[vmem, vmem],
        scratch_shapes=[pltpu.VMEM((ROWS + 8, EMB), f32)] * totals
        + [
            pltpu.VMEM((places * samples, EMB), f32),
            pltpu.SMEM((places * POOL * samples,), i32),
            pltpu.SemaphoreType.DMA,
        ],
        compiler_params=pltpu.CompilerParams(vmem_limit_bytes=38 << 20),
        name="scatter",
    )(ids, grads)


contract_last = (((1,), (1,)), ((), ()))


def dot(a, b):
    return jnp.dot(a, b, preferred_element_type=f32)


def bottom(dense, w1, w2, w3):
    def body(dense_ref, w1_ref, w2_ref, w3_ref, out_ref):
        first = jax.nn.relu(dot(dense_ref[...], w1_ref[...])).astype(bf16)
        second = jax.nn.relu(dot(first, w2_ref[...])).astype(bf16)
        out_ref[...] = jax.nn.relu(dot(second, w3_ref[...])).astype(bf16)

    return pl.pallas_call(
        body,
        out_shape=jax.ShapeDtypeStruct((dense.shape[0], EMB), bf16),
        in_specs=[vmem] * 4,
        out_specs=vmem,
        compiler_params=pltpu.CompilerParams(vmem_limit_bytes=4 << 20),
        name="bottom",
    )(dense, w1, w2, w3)


def cross(third, pooled, down, up, bias, cot):
    rows, width = cot.shape
    tables = width // EMB - 1

    def body(
        third_ref, pooled_ref, down_ref, up_ref, bias_ref, cot_ref, crossed_ref, grad_ref, stacked
    ):
        stacked[:, :EMB] = third_ref[...]
        for t in range(tables):
            stacked[:, (t + 1) * EMB : (t + 2) * EMB] = pooled_ref[t]
        low_rank = dot(stacked[...], down_ref[...]).astype(bf16)
        hidden_grad = (cot_ref[...].astype(f32) * stacked[...].astype(f32)).astype(bf16)
        low_grad = lax.dot_general(
            hidden_grad, up_ref[...], contract_last, preferred_element_type=f32
        ).astype(bf16)
        for t in range(tables + 1):
            cols = slice(t * EMB, (t + 1) * EMB)
            hidden = dot(low_rank, up_ref[:, cols]) + bias_ref[:, cols]
            wide = stacked[:, cols].astype(f32)
            crossed_ref[:, cols] = (wide * hidden + wide).astype(bf16)
            if t > 0:
                back = lax.dot_general(
                    low_grad, down_ref[cols, :], contract_last, preferred_element_type=f32
                )
                grad_ref[t - 1] = (cot_ref[:, cols].astype(f32) * (hidden + 1.0) + back).astype(
                    bf16
                )
        for t in range(tables, GROUPS):
            grad_ref[t] = jnp.zeros((rows, EMB), bf16)

    return pl.pallas_call(
        body,
        out_shape=[
            jax.ShapeDtypeStruct((rows, width), bf16),
            jax.ShapeDtypeStruct((GROUPS, rows, EMB), bf16),
        ],
        in_specs=[vmem] * 6,
        out_specs=[vmem, vmem],
        scratch_shapes=[pltpu.VMEM((rows, width), bf16)],
        compiler_params=pltpu.CompilerParams(vmem_limit_bytes=6 << 20),
        name="cross",
    )(third, pooled, down, up, bias.reshape(1, width), cot)


def per_device(
    dense_feats,
    lookup_ids,
    bag_lengths,
    bottom_w1,
    bottom_w2,
    bottom_w3,
    tables,
    accum,
    cross_down,
    cross_up,
    cross_bias,
    cotangent,
):
    samples, table_count, pool = lookup_ids.shape
    me = lax.axis_index("shard")
    my_core, my_z = me % CORES, (me // CORES) % Z_LO

    ids = jnp.transpose(lookup_ids, (1, 2, 0))
    used = jnp.arange(pool, dtype=i32)[None, :, None] < bag_lengths.T[:, None, :]
    owner, row = ids >> 6, ids & 63
    place, owner_z, owner_core = owner >> 3, (owner >> 1) & 3, owner & 1
    steps = ((owner_z - my_z) * (1 - 2 * my_core)) & 3
    address = (owner_core ^ my_core) * HALF + steps * PIECE + place * ROWS_DEV + row
    address = jnp.where(used, address, ROWS)
    digits = jnp.concatenate([address >> 7, address & 127], axis=1).astype(f32).astype(bf16)
    payload = jnp.concatenate([tables, digits], axis=1)
    payload = jnp.pad(payload, ((0, GROUPS - table_count), (0, 0), (0, 0)))
    got = exchange(payload)
    own = got[:, :ROWS_DEV].reshape(PIECE, EMB)
    high, low = got[:, ROWS_DEV : ROWS_DEV + pool], got[:, ROWS_DEV + pool :]
    at = (high.astype(f32) * 128.0 + low.astype(f32)).astype(i32).reshape(-1)

    one, three = send_z(own, -1), send_z(own, 1)
    two = send_z(one, -1)
    pieces = [own, one, two, three] + [swap(x) for x in (own, three, two, one)]
    pooled = exchange(lookup(at, pieces, samples).reshape(GROUPS, samples, EMB))

    crossed, pooled_grad = cross(
        bottom(dense_feats, bottom_w1, bottom_w2, bottom_w3),
        pooled,
        cross_down,
        cross_up,
        cross_bias,
        cotangent,
    )
    grads = exchange(pooled_grad).reshape(GROUPS * samples, EMB)
    keep, send = scatter(at, grads, samples)
    theirs = swap(send).reshape(Z_LO, PIECE, EMB)
    keep = keep.reshape(Z_LO, PIECE, EMB)

    def chip(d):
        return keep[d] + theirs[-d % Z_LO].astype(f32)

    far = send_z(chip(2).astype(bf16), -1)
    below = send_z(chip(1).astype(bf16), 1)
    above = send_z((chip(3) + far.astype(f32)).astype(bf16), -1)
    summed = (chip(0) + below.astype(f32) + above.astype(f32)).astype(bf16)
    summed = summed.reshape(GROUPS, 1, ROWS_DEV, EMB)
    halves = exchange_reps(
        jnp.broadcast_to(summed, (GROUPS, REPS, ROWS_DEV, EMB)).reshape(-1, ROWS_DEV, EMB)
    ).reshape(GROUPS, REPS, ROWS_DEV, EMB)[:table_count]
    row_grad = halves.astype(f32).sum(axis=1)
    new_accum = accum + jnp.mean(row_grad * row_grad, axis=2)
    new_tables = tables.astype(f32) - step_size * row_grad / (
        jnp.sqrt(new_accum)[:, :, None] + adagrad_eps
    )
    return crossed, new_tables, new_accum


def solution(mesh):
    in_specs = (
        P(("shard", "rep"), None),
        P(("shard", "rep"), None, None),
        P(("shard", "rep"), None),
        P(),
        P(),
        P(),
        P(None, "shard", None),
        P(None, "shard"),
        P(),
        P(),
        P(),
        P(("shard", "rep"), None),
    )
    out_specs = (P(("shard", "rep"), None), P(None, "shard", None), P(None, "shard"))
    return jax.shard_map(
        per_device, mesh=mesh, in_specs=in_specs, out_specs=out_specs, check_vma=False
    )
```

```python
import jax
import jax.numpy as jnp
from jax import lax
from jax.experimental import pallas as pl
from jax.experimental.pallas import tpu as pltpu
from jax.sharding import PartitionSpec as P

f32, bf16, i32 = jnp.float32, jnp.bfloat16, jnp.int32
step_size = 1.0
adagrad_eps = 1e-08

CORES = 2
Z_LO = 4
COLUMN = CORES * Z_LO
GROUPS = 16
SHARDS = COLUMN * GROUPS
REPS = 2
Z = Z_LO * REPS
EMB = 128
LANES = 128
POOL = 4
ROWS_DEV = 64
PIECE = GROUPS * ROWS_DEV
HALF = Z_LO * PIECE
ROWS = CORES * HALF
BITS = 14
WORDS = POOL // 2

across = [[g * COLUMN + k for g in range(GROUPS)] for k in range(COLUMN)]
across_reps = [[d * REPS + r for d in group for r in range(REPS)] for group in across]
swap_cores = [(s, s ^ 1) for s in range(SHARDS)]


def along_z(step):
    pairs = []
    for s in range(SHARDS):
        place, z_lo, core = s // COLUMN, (s // CORES) % Z_LO, s % CORES
        for r in range(REPS):
            z = (r * Z_LO + z_lo + (step if core == 0 else -step)) % Z
            target = place * COLUMN + (z % Z_LO) * CORES + core
            pairs.append((s * REPS + r, target * REPS + z // Z_LO))
    return pairs


def send_z(x, step):
    return lax.ppermute(x, ("shard", "rep"), along_z(step))


def swap(x):
    return lax.ppermute(x, "shard", swap_cores)


def exchange(x):
    return lax.all_to_all(
        x, "shard", split_axis=0, concat_axis=0, axis_index_groups=across, tiled=True
    )


def exchange_reps(x):
    return lax.all_to_all(
        x,
        ("shard", "rep"),
        split_axis=0,
        concat_axis=0,
        axis_index_groups=across_reps,
        tiled=True,
    )


vmem = pl.BlockSpec(memory_space=pltpu.VMEM)
anywhere = pl.BlockSpec(memory_space=pl.ANY)


def lookup(ids, parts, samples, unroll=128):
    count = len(parts)
    places = GROUPS

    def body(ids_any, *refs):
        part_refs, (out_ref, tab, acc, ids_ref, sem) = refs[:count], refs[count:]
        copy = pltpu.make_async_copy(ids_any, ids_ref, sem)
        copy.start()
        at = 0
        for ref in part_refs:
            tab[at : at + ref.shape[0], :] = ref[...].astype(f32)
            at += ref.shape[0]
        tab[at : at + 8, :] = jnp.zeros((8, EMB), f32)
        copy.wait()

        def place(g, _):
            def some(i, _):
                base = g * (WORDS * samples) + i * unroll
                bag = g * samples + i * unroll
                for u in range(unroll):
                    words = [ids_ref[base + (j * samples + u)] for j in range(WORDS)]
                    r = [
                        tab[pl.ds(row, 1), :]
                        for w in words
                        for row in (w & (2**BITS - 1), w >> BITS)
                    ]
                    acc[pl.ds(bag + u, 1), :] = (r[0] + r[1]) + (r[2] + r[3])
                return 0

            return lax.fori_loop(0, samples // unroll, some, 0)

        lax.fori_loop(0, places, place, 0)
        out_ref[...] = acc[...].astype(bf16)

    return pl.pallas_call(
        body,
        out_shape=jax.ShapeDtypeStruct((places * samples, EMB), bf16),
        in_specs=[anywhere] + [vmem] * count,
        out_specs=vmem,
        scratch_shapes=[
            pltpu.VMEM((ROWS + 8, EMB), f32),
            pltpu.VMEM((places * samples, EMB), f32),
            pltpu.SMEM((places * WORDS * samples,), i32),
            pltpu.SemaphoreType.DMA,
        ],
        compiler_params=pltpu.CompilerParams(vmem_limit_bytes=10 << 20),
        name="lookup",
    )(ids, *parts)


def scatter(ids, grads, samples, unroll=64):
    places, pair = GROUPS, 2
    totals = pair * POOL

    def body(ids_any, grads_ref, keep_ref, send_ref, *scratch):
        accs, (wide, ids_ref, sem) = scratch[:totals], scratch[totals:]
        copy = pltpu.make_async_copy(ids_any, ids_ref, sem)
        copy.start()
        for a in accs:
            a[...] = jnp.zeros((ROWS + 8, EMB), f32)
        wide[...] = grads_ref[...].astype(f32)
        copy.wait()

        def place(g, _):
            def some(i, _):
                base = g * (POOL * samples) + i * unroll
                bag = g * samples + i * unroll
                for u in range(0, unroll, pair):
                    row = [wide[pl.ds(bag + (u + k), 1), :] for k in range(pair)]
                    at = [
                        ids_ref[base + (j * samples + u + k)]
                        for k in range(pair)
                        for j in range(POOL)
                    ]
                    new = [
                        accs[n][pl.ds(at[n], 1), :] + row[n // POOL] for n in range(totals)
                    ]
                    for n in range(totals):
                        accs[n][pl.ds(at[n], 1), :] = new[n]
                return 0

            return lax.fori_loop(0, samples // unroll, some, 0)

        lax.fori_loop(0, places, place, 0)
        block = 256

        def total(at):
            sl = pl.ds(pl.multiple_of(at, block), block)
            t = [a[sl, :] for a in accs]
            while len(t) > 1:
                t = [t[2 * k] + t[2 * k + 1] for k in range(len(t) // 2)]
            return t[0]

        def finish(i, _):
            sl = pl.ds(pl.multiple_of(i * block, block), block)
            send_ref[sl, :] = total(HALF + i * block).astype(bf16)
            keep_ref[sl, :] = total(i * block)
            return 0

        lax.fori_loop(0, HALF // block, finish, 0)

    return pl.pallas_call(
        body,
        out_shape=[
            jax.ShapeDtypeStruct((HALF, EMB), f32),
            jax.ShapeDtypeStruct((HALF, EMB), bf16),
        ],
        in_specs=[anywhere, vmem],
        out_specs=[vmem, vmem],
        scratch_shapes=[pltpu.VMEM((ROWS + 8, EMB), f32)] * totals
        + [
            pltpu.VMEM((places * samples, EMB), f32),
            pltpu.SMEM((places * POOL * samples,), i32),
            pltpu.SemaphoreType.DMA,
        ],
        compiler_params=pltpu.CompilerParams(vmem_limit_bytes=38 << 20),
        name="scatter",
    )(ids, grads)


contract_last = (((1,), (1,)), ((), ()))


def dot(a, b):
    return jnp.dot(a, b, preferred_element_type=f32)


def bottom(dense, w1, w2, w3):
    def body(dense_ref, w1_ref, w2_ref, w3_ref, out_ref):
        first = jax.nn.relu(dot(dense_ref[...], w1_ref[...])).astype(bf16)
        second = jax.nn.relu(dot(first, w2_ref[...])).astype(bf16)
        out_ref[...] = jax.nn.relu(dot(second, w3_ref[...])).astype(bf16)

    return pl.pallas_call(
        body,
        out_shape=jax.ShapeDtypeStruct((dense.shape[0], EMB), bf16),
        in_specs=[vmem] * 4,
        out_specs=vmem,
        compiler_params=pltpu.CompilerParams(vmem_limit_bytes=4 << 20),
        name="bottom",
    )(dense, w1, w2, w3)


def cross(third, pooled, down, up, bias, cot):
    rows, width = cot.shape
    tables = width // EMB - 1

    def body(
        third_ref, pooled_ref, down_ref, up_ref, bias_ref, cot_ref, crossed_ref, grad_ref, stacked
    ):
        stacked[:, :EMB] = third_ref[...]
        for t in range(tables):
            stacked[:, (t + 1) * EMB : (t + 2) * EMB] = pooled_ref[t]
        low_rank = dot(stacked[...], down_ref[...]).astype(bf16)
        hidden_grad = (cot_ref[...].astype(f32) * stacked[...].astype(f32)).astype(bf16)
        low_grad = lax.dot_general(
            hidden_grad, up_ref[...], contract_last, preferred_element_type=f32
        ).astype(bf16)
        for t in range(tables + 1):
            cols = slice(t * EMB, (t + 1) * EMB)
            hidden = dot(low_rank, up_ref[:, cols]) + bias_ref[:, cols]
            wide = stacked[:, cols].astype(f32)
            crossed_ref[:, cols] = (wide * hidden + wide).astype(bf16)
            if t > 0:
                back = lax.dot_general(
                    low_grad, down_ref[cols, :], contract_last, preferred_element_type=f32
                )
                grad_ref[t - 1] = (cot_ref[:, cols].astype(f32) * (hidden + 1.0) + back).astype(
                    bf16
                )
        for t in range(tables, GROUPS):
            grad_ref[t] = jnp.zeros((rows, EMB), bf16)

    return pl.pallas_call(
        body,
        out_shape=[
            jax.ShapeDtypeStruct((rows, width), bf16),
            jax.ShapeDtypeStruct((GROUPS, rows, EMB), bf16),
        ],
        in_specs=[vmem] * 6,
        out_specs=[vmem, vmem],
        scratch_shapes=[pltpu.VMEM((rows, width), bf16)],
        compiler_params=pltpu.CompilerParams(vmem_limit_bytes=6 << 20),
        name="cross",
    )(third, pooled, down, up, bias.reshape(1, width), cot)


def per_device(
    dense_feats,
    lookup_ids,
    bag_lengths,
    bottom_w1,
    bottom_w2,
    bottom_w3,
    tables,
    accum,
    cross_down,
    cross_up,
    cross_bias,
    cotangent,
):
    samples, table_count, pool = lookup_ids.shape
    me = lax.axis_index("shard")
    my_core, my_z = me % CORES, (me // CORES) % Z_LO

    ids = jnp.transpose(lookup_ids, (1, 2, 0))
    used = jnp.arange(pool, dtype=i32)[None, :, None] < bag_lengths.T[:, None, :]
    owner, row = ids >> 6, ids & 63
    place, owner_z, owner_core = owner >> 3, (owner >> 1) & 3, owner & 1
    steps = ((owner_z - my_z) * (1 - 2 * my_core)) & 3
    address = (owner_core ^ my_core) * HALF + steps * PIECE + place * ROWS_DEV + row
    address = jnp.where(used, address, ROWS)
    digits = jnp.concatenate([address >> 7, address & 127], axis=1).astype(f32).astype(bf16)
    payload = jnp.concatenate([tables, digits], axis=1)
    payload = jnp.pad(payload, ((0, GROUPS - table_count), (0, 0), (0, 0)))
    got = exchange(payload)
    own = got[:, :ROWS_DEV].reshape(PIECE, EMB)
    high, low = got[:, ROWS_DEV : ROWS_DEV + pool], got[:, ROWS_DEV + pool :]
    at = (high.astype(f32) * 128.0 + low.astype(f32)).astype(i32)
    words = (at[:, :WORDS] | at[:, WORDS:] << BITS).reshape(-1)
    at = at.reshape(-1)

    one, three = send_z(own, -1), send_z(own, 1)
    two = send_z(one, -1)
    pieces = [own, one, two, three] + [swap(x) for x in (own, three, two, one)]
    pooled = exchange(lookup(words, pieces, samples).reshape(GROUPS, samples, EMB))

    crossed, pooled_grad = cross(
        bottom(dense_feats, bottom_w1, bottom_w2, bottom_w3),
        pooled,
        cross_down,
        cross_up,
        cross_bias,
        cotangent,
    )
    grads = exchange(pooled_grad).reshape(GROUPS * samples, EMB)
    keep, send = scatter(at, grads, samples)
    theirs = swap(send).reshape(Z_LO, PIECE, EMB)
    keep = keep.reshape(Z_LO, PIECE, EMB)

    def chip(d):
        return keep[d] + theirs[-d % Z_LO].astype(f32)

    far = send_z(chip(2).astype(bf16), -1)
    below = send_z(chip(1).astype(bf16), 1)
    above = send_z((chip(3) + far.astype(f32)).astype(bf16), -1)
    summed = (chip(0) + below.astype(f32) + above.astype(f32)).astype(bf16)
    summed = summed.reshape(GROUPS, 1, ROWS_DEV, EMB)
    halves = exchange_reps(
        jnp.broadcast_to(summed, (GROUPS, REPS, ROWS_DEV, EMB)).reshape(-1, ROWS_DEV, EMB)
    ).reshape(GROUPS, REPS, ROWS_DEV, EMB)[:table_count]
    row_grad = halves.astype(f32).sum(axis=1)
    new_accum = accum + jnp.mean(row_grad * row_grad, axis=2)
    new_tables = tables.astype(f32) - step_size * row_grad / (
        jnp.sqrt(new_accum)[:, :, None] + adagrad_eps
    )
    return crossed, new_tables, new_accum


def solution(mesh):
    in_specs = (
        P(("shard", "rep"), None),
        P(("shard", "rep"), None, None),
        P(("shard", "rep"), None),
        P(),
        P(),
        P(),
        P(None, "shard", None),
        P(None, "shard"),
        P(),
        P(),
        P(),
        P(("shard", "rep"), None),
    )
    out_specs = (P(("shard", "rep"), None), P(None, "shard", None), P(None, "shard"))
    return jax.shard_map(
        per_device, mesh=mesh, in_specs=in_specs, out_specs=out_specs, check_vma=False
    )
```
